32 devices in a mesh: grp: 2 (over y), gx: 4 (over z), gy: 2 (over x), gz: 2 (over core).
Axes of the slice: x: 2, y: 2, z: 4, core: 2. Of those that a mesh axis runs over, the one named last changes fastest.
Arguments:
- coef_start: float32 [81, 8, 2, 2, 128], P(None, ('grp', 'gx'), 'gy', 'gz'), parts along dimension 1, may hold values from -6 to 6
- dipole_start: float32 [3, 8, 2, 2, 128], P(None, ('grp', 'gx'), 'gy', 'gz'), parts along dimension 1, may hold values from -4 to 4
- source: float32 [81, 8, 2, 2, 128], P(None, ('grp', 'gx'), 'gy', 'gz'), parts along dimension 1, may hold values from -6 to 6
- indicator: float32 [302, 8, 2, 2, 128], P(None, ('grp', 'gx'), 'gy', 'gz'), parts along dimension 1, may hold values from 0 to 1
- polarity: float32 [8, 2, 2, 128], P(('grp', 'gx'), 'gy', 'gz'), parts along dimension 0, may hold values from 0.2 to 1
- external: float32 [3, 8, 2, 2, 128], P(None, ('grp', 'gx'), 'gy', 'gz'), parts along dimension 1, may hold values from -6 to 6
- counts: int32 [8, 2, 2], P(('grp', 'gx'), 'gy', 'gz'), parts along dimension 0, may hold values from 32 to 128, as said below
- cosmo_index: int32 [16, 8, 2, 2, 128], P(None, ('grp', 'gx'), 'gy', 'gz'), parts along dimension 1, may hold values from 0 to 991, as said below
- cosmo_weight: float32 [16, 8, 2, 2, 128], P(None, ('grp', 'gx'), 'gy', 'gz'), parts along dimension 1, may hold values from 0 to 0.08
- cosmo_dist: float32 [16, 8, 2, 2, 128], P(None, ('grp', 'gx'), 'gy', 'gz'), parts along dimension 1, may hold values from 1 to 3
- cosmo_theta: float32 [16, 8, 2, 2, 128], P(None, ('grp', 'gx'), 'gy', 'gz'), parts along dimension 1, may hold values from 0 to 3.14159
- cosmo_phi: float32 [16, 8, 2, 2, 128], P(None, ('grp', 'gx'), 'gy', 'gz'), parts along dimension 1, may hold values from -3.140625 to 3.140625
- thole_index: int32 [16, 8, 2, 2, 128], P(None, ('grp', 'gx'), 'gy', 'gz'), parts along dimension 1, may hold values from 0 to 991, as said below
- thole_weight: float32 [16, 8, 2, 2, 128], P(None, ('grp', 'gx'), 'gy', 'gz'), parts along dimension 1, may hold values from 0 to 0.5
- thole_dist: float32 [16, 8, 2, 2, 128], P(None, ('grp', 'gx'), 'gy', 'gz'), parts along dimension 1, may hold values from 1 to 3
- thole_theta: float32 [16, 8, 2, 2, 128], P(None, ('grp', 'gx'), 'gy', 'gz'), parts along dimension 1, may hold values from 0 to 3.14159
- thole_phi: float32 [16, 8, 2, 2, 128], P(None, ('grp', 'gx'), 'gy', 'gz'), parts along dimension 1, may hold values from -3.140625 to 3.140625
- harmonics: float32 [302, 81], replicated, may hold values from -6 to 6
- lebedev: float32 [302], replicated, may hold values from 0.03 to 0.055
Outputs:
- coefficients: float32 [81, 8, 2, 2, 128], P(None, ('grp', 'gx'), 'gy', 'gz'), parts along dimension 1
- dipoles: float32 [3, 8, 2, 2, 128], P(None, ('grp', 'gx'), 'gy', 'gz'), parts along dimension 1
The draws below stay inside these ranges and needn't reach their ends.
There are 2 independent parts, one for each index of `grp`. The reference program is written for one: setup_inputs(seed, part) draws one part's arguments, and reference() takes and returns one part's arrays. A program takes and returns all parts, laid end to end along the dimension named above; an argument that names none is the same for every part. Nothing has to cross between parts.
Inputs may be any that keep to these rules, and one draw needn't show every extreme that they name: `counts`: the live spheres of a domain are its leading slots and include all 32 slots that neighbours may reference; some domain is full and some holds only 32. `cosmo_index`: a column of the domain's pool as laid out in the reference program; spheres in slots 32 and up name only columns of their own domain. `thole_index`: a column of the domain's pool as laid out in the reference program; atoms in slots 32 and up name only columns of their own domain.
All inputs are finite; a program needn't handle non-finite values.
Results may differ from the reference program's by a relative error of at most 0.0003.
Values sent between devices are 32-bit elements; how exact they have to be, the bound alone decides.
A program may use at most 64 MiB of HBM per device.

```python
import math
import jax
import jax.numpy as jnp
from jax import lax

COEF = 81
GRID = 302
SPH_DEV = 128
BORDER = 32
NBR = 16
TPAIR = 16
ITERS = 3
DOM_X = 4
DOM_Y = 2
DOM_Z = 2


def draw_counts(key, part):
    key = jax.random.fold_in(key, 7)
    key_counts, key_order = jax.random.split(key)
    dom_total = DOM_X * DOM_Y * DOM_Z
    drawn = jax.random.randint(key_counts, (dom_total,), BORDER, SPH_DEV + 1)
    order_perm = jax.random.permutation(key_order, dom_total)
    drawn = drawn.at[order_perm[0]].set(SPH_DEV).at[order_perm[1]].set(BORDER)
    return drawn.reshape(DOM_X, DOM_Y, DOM_Z).astype(jnp.int32)


def pool_columns(key, slots):
    key_own, key_offset, key_within, key_remote = jax.random.split(key, 4)
    shape = (slots, DOM_X, DOM_Y, DOM_Z, SPH_DEV)
    own = jax.random.randint(key_own, shape, 27 * BORDER, 27 * BORDER + SPH_DEV)
    ticket = jax.random.randint(key_offset, shape, 0, 80)
    offset = jnp.zeros(shape, jnp.int32)
    running = 0
    for block in range(27):
        spread_x = block // 9 - 1
        spread_y = block // 3 % 3 - 1
        spread_z = block % 3 - 1
        moved = abs(spread_x) + abs(spread_y) + abs(spread_z)
        share = [0, 8, 2, 1][moved]
        running = running + share
        if block < 26:
            offset = offset + (ticket >= running).astype(jnp.int32)
    within = jax.random.randint(key_within, shape, 0, BORDER)
    remote_col = offset * BORDER + within
    slot_index = jnp.arange(SPH_DEV, dtype=jnp.int32)
    remote_flag = (jax.random.randint(key_remote, shape, 0, 2) == 1) & (slot_index < BORDER)
    chosen = jnp.where(remote_flag, remote_col, own)
    chosen = chosen.at[0, 0, 0, 0, 0].set(0)
    chosen = chosen.at[0, 0, 0, 0, BORDER].set(27 * BORDER + SPH_DEV - 1)
    return chosen.astype(jnp.int32)


def draw_cosmo_index(key, part):
    key = jax.random.fold_in(key, 11)
    return pool_columns(key, NBR)


def draw_thole_index(key, part):
    key = jax.random.fold_in(key, 13)
    return pool_columns(key, TPAIR)


def block_scale(own_key, dims, cuts, low, high):
    factor_of, own = 1.0, jax.random.fold_in(own_key, 6)
    for position, shards_of in cuts:
        draws = jnp.exp(jax.random.uniform(jax.random.fold_in(own, position), (shards_of,), jnp.float32, low / len(cuts), high / len(cuts)))
        factor_of = factor_of * jnp.repeat(draws, dims[position] // shards_of).reshape([-1 if axis == position else 1 for axis in range(len(dims))])
    return factor_of


def gaussian(own_key, shape, deviation, most, cuts=(), held_as=jnp.bfloat16):
    array = jax.random.normal(own_key, shape, jnp.float32) * deviation
    if len(cuts) > 0:
        array = block_scale(own_key, shape, cuts, -0.22, 0.18) * array
    return jnp.clip(array, min=-most, max=most).astype(held_as)


def setup_inputs(seed: int = 0, part: int = 0) -> dict:
    keys = jax.random.split(jax.random.key(seed), 20)
    part_splits = jax.random.split(jax.random.fold_in(keys[19], part), 20)
    return {
        "coef_start": gaussian(part_splits[0], (COEF, DOM_X, DOM_Y, DOM_Z, SPH_DEV), 1.0, 6.0, ((1, 4), (2, 2), (3, 2)), jnp.float32),
        "dipole_start": gaussian(part_splits[1], (3, DOM_X, DOM_Y, DOM_Z, SPH_DEV), 0.5, 4.0, ((1, 4), (2, 2), (3, 2)), jnp.float32),
        "source": gaussian(part_splits[2], (COEF, DOM_X, DOM_Y, DOM_Z, SPH_DEV), 1.0, 6.0, ((1, 4), (2, 2), (3, 2)), jnp.float32),
        "indicator": jnp.clip(1.0 * jax.random.uniform(part_splits[3], (GRID, DOM_X, DOM_Y, DOM_Z, SPH_DEV), jnp.float32) ** block_scale(part_splits[3], (GRID, DOM_X, DOM_Y, DOM_Z, SPH_DEV), ((1, 4), (2, 2), (3, 2)), -0.2, 0.2), 0.0, 1.0),
        "polarity": jnp.clip(jnp.exp(math.log(1.0) - 1.609438 * jax.random.uniform(part_splits[4], (DOM_X, DOM_Y, DOM_Z, SPH_DEV), jnp.float32) ** block_scale(part_splits[4], (DOM_X, DOM_Y, DOM_Z, SPH_DEV), ((0, 4), (1, 2), (2, 2)), -0.2, 0.2)), 0.2, 1.0),
        "external": gaussian(part_splits[5], (3, DOM_X, DOM_Y, DOM_Z, SPH_DEV), 1.0, 6.0, ((1, 4), (2, 2), (3, 2)), jnp.float32),
        "counts": draw_counts(jax.random.fold_in(jax.random.fold_in(keys[19], part), 71), part),
        "cosmo_index": draw_cosmo_index(jax.random.fold_in(jax.random.fold_in(keys[19], part), 71), part),
        "cosmo_weight": jnp.clip(0.08 * jax.random.uniform(part_splits[8], (NBR, DOM_X, DOM_Y, DOM_Z, SPH_DEV), jnp.float32) ** block_scale(part_splits[8], (NBR, DOM_X, DOM_Y, DOM_Z, SPH_DEV), ((1, 4), (2, 2), (3, 2)), -0.2, 0.2), 0.0, 0.08),
        "cosmo_dist": jnp.clip(jnp.exp(math.log(3.0) - 1.0986123 * jax.random.uniform(part_splits[9], (NBR, DOM_X, DOM_Y, DOM_Z, SPH_DEV), jnp.float32) ** block_scale(part_splits[9], (NBR, DOM_X, DOM_Y, DOM_Z, SPH_DEV), ((1, 4), (2, 2), (3, 2)), -0.2, 0.2)), 1.0, 3.0),
        "cosmo_theta": jnp.clip(3.14159 * jax.random.uniform(part_splits[10], (NBR, DOM_X, DOM_Y, DOM_Z, SPH_DEV), jnp.float32) ** block_scale(part_splits[10], (NBR, DOM_X, DOM_Y, DOM_Z, SPH_DEV), ((1, 4), (2, 2), (3, 2)), -0.2, 0.2), 0.0, 3.14159),
        "cosmo_phi": jnp.clip(jax.random.uniform(part_splits[11], (NBR, DOM_X, DOM_Y, DOM_Z, SPH_DEV), jnp.float32, -3.140625, 3.140625), -3.140625, 3.140625),
        "thole_index": draw_thole_index(jax.random.fold_in(jax.random.fold_in(keys[19], part), 71), part),
        "thole_weight": jnp.clip(0.5 * jax.random.uniform(part_splits[13], (TPAIR, DOM_X, DOM_Y, DOM_Z, SPH_DEV), jnp.float32) ** block_scale(part_splits[13], (TPAIR, DOM_X, DOM_Y, DOM_Z, SPH_DEV), ((1, 4), (2, 2), (3, 2)), -0.2, 0.2), 0.0, 0.5),
        "thole_dist": jnp.clip(jnp.exp(math.log(3.0) - 1.0986123 * jax.random.uniform(part_splits[14], (TPAIR, DOM_X, DOM_Y, DOM_Z, SPH_DEV), jnp.float32) ** block_scale(part_splits[14], (TPAIR, DOM_X, DOM_Y, DOM_Z, SPH_DEV), ((1, 4), (2, 2), (3, 2)), -0.2, 0.2)), 1.0, 3.0),
        "thole_theta": jnp.clip(3.14159 * jax.random.uniform(part_splits[15], (TPAIR, DOM_X, DOM_Y, DOM_Z, SPH_DEV), jnp.float32) ** block_scale(part_splits[15], (TPAIR, DOM_X, DOM_Y, DOM_Z, SPH_DEV), ((1, 4), (2, 2), (3, 2)), -0.2, 0.2), 0.0, 3.14159),
        "thole_phi": jnp.clip(jax.random.uniform(part_splits[16], (TPAIR, DOM_X, DOM_Y, DOM_Z, SPH_DEV), jnp.float32, -3.140625, 3.140625), -3.140625, 3.140625),
        "harmonics": gaussian(keys[17], (GRID, COEF), 1.0, 6.0, (), jnp.float32),
        "lebedev": jnp.clip(jax.random.uniform(keys[18], (GRID,), jnp.float32, 0.03, 0.055), 0.03, 0.055),
    }


PRECISE = lax.Precision.HIGHEST
THOLE_DAMPING = 0.39
INJECT_SCALE = 2.0
RADIUS_SCALE = 0.9

def degree_table(coef_total):
    row_index = jnp.arange(coef_total)
    squares = jnp.arange(1, math.isqrt(coef_total)) ** 2
    return lax.optimization_barrier(jnp.sum((row_index[:, None] >= squares[None, :]).astype(jnp.float32), axis=1))

def unit_vectors(polar_angle, azimuth):
    sin_theta = jnp.sin(polar_angle)
    return jnp.stack([sin_theta * jnp.cos(azimuth), sin_theta * jnp.sin(azimuth), jnp.cos(polar_angle)])

def domain_update(candidates, coeffs, dipoles, source, indicator, external, cosmo_index, cosmo_weight, cosmo_dist, cosmo_theta, cosmo_phi, thole_index, thole_weight, thole_dist, thole_theta, thole_phi, harmonics, lebedev, living):
    coef_count = coeffs.shape[0]
    sphere_count = coeffs.shape[1]
    degree_rows = degree_table(coef_count)
    neighbours = jnp.take(candidates[:coef_count], cosmo_index, axis=1)
    ratio_log = jnp.log(RADIUS_SCALE / cosmo_dist)
    radial = jnp.exp(degree_rows[:, None, None] * ratio_log[None])
    coupled = lax.optimization_barrier(jnp.sum(cosmo_weight[None] * radial * neighbours, axis=1))
    stacked = jnp.concatenate([coupled, coeffs], axis=1)
    values = jnp.dot(harmonics, stacked, precision=PRECISE, preferred_element_type=jnp.float32)
    density = lebedev[:, None] * indicator
    weighted = values * jnp.concatenate([density, density], axis=1)
    projected = lax.dot_general(harmonics, weighted, (((0,), (0,)), ((), ())), precision=PRECISE, preferred_element_type=jnp.float32)
    scaled = (2.0 * degree_rows + 1.0) / (4.0 * math.pi)
    injected = source + jnp.pad(INJECT_SCALE * dipoles, ((1, coef_count - 4), (0, 0)))
    new_coeffs = living[None, :] * scaled[:, None] * (injected - projected[:, :sphere_count])
    moment = projected[1:4, sphere_count:]
    cosmo_dirs = unit_vectors(cosmo_theta, cosmo_phi)
    along_axis = lax.optimization_barrier(jnp.sum(cosmo_dirs * moment[:, None, :], axis=0))
    strength = cosmo_weight / cosmo_dist ** 3
    partial_field = strength[None] * (3.0 * cosmo_dirs * along_axis[None] - moment[:, None, :])
    flat_field = partial_field.reshape(3, -1).T
    pushed = jax.ops.segment_sum(flat_field, cosmo_index.reshape(-1), num_segments=candidates.shape[1]).T
    partner = jnp.take(candidates[coef_count:], thole_index, axis=1)
    thole_dirs = unit_vectors(thole_theta, thole_phi)
    dist_cubed = thole_dist ** 3
    screen = jnp.exp(-THOLE_DAMPING * dist_cubed)
    lambda_three = 1.0 - screen
    lambda_five = 1.0 - (1.0 + THOLE_DAMPING * dist_cubed) * screen
    projection = lax.optimization_barrier(jnp.sum(thole_dirs * partner, axis=0))
    tensor_part = 3.0 * lambda_five[None] * thole_dirs * projection[None] - lambda_three[None] * partner
    induced = lax.optimization_barrier(jnp.sum((thole_weight / dist_cubed)[None] * tensor_part, axis=1))
    return (new_coeffs, pushed, induced)

def domains_first(values_in):
    moved = jnp.moveaxis(values_in, 0, 3)
    return moved.reshape((-1,) + moved.shape[3:])

def domains_back(values_in):
    shaped = values_in.reshape((DOM_X, DOM_Y, DOM_Z) + values_in.shape[1:])
    return jnp.moveaxis(shaped, 3, 0)

def reference(coef_start, dipole_start, source, indicator, polarity, external, counts, cosmo_index, cosmo_weight, cosmo_dist, cosmo_theta, cosmo_phi, thole_index, thole_weight, thole_dist, thole_theta, thole_phi, harmonics, lebedev):
    dom_total = DOM_X * DOM_Y * DOM_Z
    live_flat = (jnp.arange(SPH_DEV, dtype=jnp.int32)[None, :] < counts.reshape(-1)[:, None]).astype(jnp.float32)
    live_grid = live_flat.reshape(DOM_X, DOM_Y, DOM_Z, SPH_DEV)
    source_flat = domains_first(source)
    indicator_flat = domains_first(indicator)
    external_flat = domains_first(external)
    cindex_flat = domains_first(cosmo_index)
    cweight_flat = domains_first(cosmo_weight)
    cdist_flat = domains_first(cosmo_dist)
    ctheta_flat = domains_first(cosmo_theta)
    cphi_flat = domains_first(cosmo_phi)
    tindex_flat = domains_first(thole_index)
    tweight_flat = domains_first(thole_weight)
    tdist_flat = domains_first(thole_dist)
    ttheta_flat = domains_first(thole_theta)
    tphi_flat = domains_first(thole_phi)
    coeffs = coef_start
    dipoles = dipole_start
    state_rows = COEF + 3
    for sweep_index in range(ITERS):
        current = jnp.concatenate([coeffs, dipoles], axis=0)
        padded = jnp.pad(current[..., :BORDER], ((0, 0), (1, 1), (1, 1), (1, 1), (0, 0)))
        own_state = domains_first(current)

        def one_domain(domain_index):
            index_x = domain_index // (DOM_Y * DOM_Z)
            index_y = domain_index // DOM_Z % DOM_Y
            index_z = domain_index % DOM_Z
            zero_start = jnp.zeros((), jnp.int32)
            nearby = lax.dynamic_slice(padded, (zero_start, index_x, index_y, index_z, zero_start), (state_rows, 3, 3, 3, BORDER))
            candidates = jnp.concatenate([nearby.reshape(state_rows, 27 * BORDER), own_state[domain_index]], axis=1)
            return domain_update(candidates, own_state[domain_index][:COEF], own_state[domain_index][COEF:], source_flat[domain_index], indicator_flat[domain_index], external_flat[domain_index], cindex_flat[domain_index], cweight_flat[domain_index], cdist_flat[domain_index], ctheta_flat[domain_index], cphi_flat[domain_index], tindex_flat[domain_index], tweight_flat[domain_index], tdist_flat[domain_index], ttheta_flat[domain_index], tphi_flat[domain_index], harmonics, lebedev, live_flat[domain_index])
        new_all, pushed_all, induced_all = lax.map(one_domain, jnp.arange(dom_total, dtype=jnp.int32))
        pushed_blocks = pushed_all[:, :, :27 * BORDER].reshape(DOM_X, DOM_Y, DOM_Z, 3, 3, 3, 3, BORDER)
        gathered = jnp.zeros((3, DOM_X + 2, DOM_Y + 2, DOM_Z + 2, BORDER), jnp.float32)
        for step_x in range(3):
            for step_y in range(3):
                for step_z in range(3):
                    piece = jnp.moveaxis(pushed_blocks[:, :, :, :, step_x, step_y, step_z, :], 3, 0)
                    gathered = gathered.at[:, step_x:step_x + DOM_X, step_y:step_y + DOM_Y, step_z:step_z + DOM_Z, :].add(piece)
        border_sum = gathered[:, 1:-1, 1:-1, 1:-1, :]
        own_back = domains_back(pushed_all[:, :, 27 * BORDER:])
        field_back = own_back + jnp.pad(border_sum, ((0, 0), (0, 0), (0, 0), (0, 0), (0, SPH_DEV - BORDER)))
        coeffs = domains_back(new_all)
        induced_grid = domains_back(induced_all)
        dipoles = live_grid[None] * polarity[None] * (external + induced_grid + field_back)
    return (coeffs, dipoles)
```

```python
import functools
import itertools
import math

import jax
import jax.numpy as jnp
from jax import lax
from jax.experimental import pallas as pl
from jax.experimental.pallas import tpu as pltpu
from jax.sharding import PartitionSpec as P

ITERS = 3
AXES = ("gx", "gy", "gz")
MESH = pl.DeviceIdType.MESH
THOLE_DAMPING = 0.39
INJECT_SCALE = 2.0
RADIUS_SCALE = 0.9

COEF = 81
GRID = 302
LANES = 128
BORDER = 32
PAIRS = 16
GROUPS = LANES // BORDER
PACK = 24
ROWS = GROUPS * PACK
CROWS = 88
GRID_PAD = 304
GRID_K = 384
F32 = jnp.float32
BF16 = jnp.bfloat16


def axis_digits(size):
    if size >= 3:
        return (-1, 0, 1)
    return (0, 1) if size == 2 else (0,)


class Slots:
    def __init__(self, sizes):
        self.sizes = sizes
        self.digits = [axis_digits(n) for n in sizes]
        self.all = list(itertools.product(*[range(len(d)) for d in self.digits]))
        self.count = len(self.all)
        self.tiles = -(-self.count // GROUPS)
        centre = tuple(d.index(0) for d in self.digits)
        self.own = self.all.index(centre)
        self.others = [i for i in range(self.count) if i != self.own]

    def mirror(self, slot):
        place = self.all[slot]
        back = tuple(2 - e if n >= 3 else e for e, n in zip(place, self.sizes))
        return self.all.index(back)

    def device(self, slot, me):
        ids = {}
        for axis, n, d, e, i in zip(AXES, self.sizes, self.digits, self.all[slot], me):
            if d[e] == 0:
                continue
            ids[axis] = i + d[e] if n >= 3 else 1 - i
        return ids

    def valid(self, slot, me):
        cond = None
        for n, d, e, i in zip(self.sizes, self.digits, self.all[slot], me):
            if n < 3 or d[e] == 0:
                continue
            here = (i + d[e] >= 0) & (i + d[e] < n)
            cond = here if cond is None else cond & here
        return cond


def when(cond, fn):
    if cond is None:
        fn()
    else:
        pl.when(cond)(fn)


def lane_group(shape):
    return lax.broadcasted_iota(jnp.int32, shape, len(shape) - 1) >> 5


def lane_take(table, lanes):
    return jnp.take_along_axis(table, lanes, axis=1, mode="promise_in_bounds")


def rolled(x, shift):
    shift = shift % LANES
    return x if shift == 0 else pltpu.roll(x, shift, 1)


def degree_rows(rows):
    row = lax.broadcasted_iota(jnp.int32, (rows, LANES), 0)
    total = jnp.zeros((rows, LANES), F32)
    for level in range(1, math.isqrt(COEF)):
        total = total + jnp.where(row >= level * level, 1.0, 0.0)
    return total


def split(x):
    high = x.astype(BF16)
    return high, (x - high.astype(F32)).astype(BF16)


def columns(index, me, plan):
    block = index >> 5
    within = index & 31
    bx = (block * 57) >> 9
    rest = block - 9 * bx
    by = (rest * 171) >> 9
    bz = rest - 3 * by
    inside = None
    slot = jnp.zeros_like(index)
    for n, d, b, i in zip(plan.sizes, plan.digits, (bx, by, bz), me):
        step = b - 1
        here = (step + i >= 0) & (step + i < n)
        inside = here if inside is None else inside & here
        digit = b if n >= 3 else step * step
        slot = slot * len(d) + (digit if n >= 2 else jnp.zeros_like(index))
    remote = jnp.where(inside, LANES + slot * BORDER + within, -1)
    column = jnp.where(block == 13, within, remote)
    return jnp.where(index >= 27 * BORDER, index - 27 * BORDER, column)


def kernel(
    plan,
    coef_ref, dip_ref, source_ref, ind_ref, polar_ref, ext_ref, counts_ref,
    cidx_ref, cw_ref, cd_ref, ct_ref, cp_ref,
    tidx_ref, tw_ref, td_ref, tt_ref, tp_ref,
    harm_ref, leb_ref,
    coef_out, dip_out,
    cs, ds, src, inj, ext, tmp, sbuf, cbuf, fdbuf, fdrecv,
    colb, pk, wr, wrp, edir, edirp, stren, ohown, ohrem, fown, frem,
    hk, ht, htm, hsq, zs, ws, ind, thc, pool,
    csend, crecv, fsend, frecv,
):
    me = tuple(lax.axis_index(a) for a in AXES)
    group24 = lane_group((PACK, LANES))
    group8 = lane_group((8, LANES))
    iota8 = lax.broadcasted_iota(jnp.int32, (8, LANES), 0)

    cs[...] = jnp.zeros_like(cs)
    ds[...] = jnp.zeros_like(ds)
    cs[0:COEF, :] = coef_ref[...]
    ds[0:3, :] = dip_ref[...]
    for slot in plan.others:
        cond = plan.valid(slot, me)
        if cond is not None:
            def clear(slot=slot):
                for s in range(ITERS):
                    cbuf[s, slot] = jnp.zeros((PACK, LANES), F32)
                    fdrecv[s, slot] = jnp.zeros((8, LANES), F32)
            pl.when(jnp.logical_not(cond))(clear)

    barrier = pltpu.get_barrier_semaphore()
    number = 0
    for slot in plan.others:
        cond = plan.valid(slot, me)
        ids = plan.device(slot, me)
        when(cond, lambda ids=ids: pl.semaphore_signal(barrier, inc=1, device_id=ids, device_id_type=MESH))
        number = number + (1 if cond is None else cond.astype(jnp.int32))

    def c_copy(s, slot, arriving=False):
        back = slot if arriving else plan.mirror(slot)
        return pltpu.make_async_remote_copy(
            src_ref=sbuf.at[s], dst_ref=cbuf.at[s, back],
            send_sem=csend.at[s, slot], recv_sem=crecv.at[s, back],
            device_id=plan.device(slot, me), device_id_type=MESH,
        )

    def f_copy(s, slot, arriving=False):
        back = slot if arriving else plan.mirror(slot)
        return pltpu.make_async_remote_copy(
            src_ref=fdbuf.at[s, slot // GROUPS], dst_ref=fdrecv.at[s, back],
            send_sem=fsend.at[s, slot], recv_sem=frecv.at[s, back],
            device_id=plan.device(slot, me), device_id_type=MESH,
        )

    def each(make, s, act):
        for slot in plan.others:
            when(plan.valid(slot, me), lambda slot=slot: act(make(s, slot)))

    def arrive(make, s):
        for slot in plan.others:
            when(plan.valid(slot, me), lambda slot=slot: make(s, slot, True).wait_recv())

    def pack_coefs(s):
        packed = cs[0:PACK, :]
        for j in range(1, GROUPS):
            packed = jnp.where(group24 == j, rolled(cs[j * PACK:(j + 1) * PACK, :], BORDER * j), packed)
        sbuf[s] = packed

    pack_coefs(0)
    pl.semaphore_wait(barrier, number)
    each(c_copy, 0, lambda c: c.start())

    zero8 = jnp.zeros((8, LANES), F32)
    src[...] = jnp.zeros_like(src)
    src[0:COEF, :] = source_ref[...]
    inj[...] = jnp.zeros_like(inj)
    ext[...] = zero8
    ext[0:3, :] = ext_ref[...]
    tmp[...] = zero8
    ind[...] = jnp.zeros_like(ind)
    ind[0:GRID, :] = ind_ref[...]
    zs[...] = jnp.zeros_like(zs)
    ws[...] = jnp.zeros_like(ws)
    hsq[...] = jnp.zeros_like(hsq)
    hsq[0:GRID, 0:COEF] = harm_ref[...]
    pk[...] = jnp.zeros_like(pk)
    colb[...] = jnp.zeros_like(colb)
    edir[...] = jnp.zeros_like(edir)
    edirp[...] = jnp.zeros_like(edirp)
    stren[...] = jnp.zeros_like(stren)

    def project_tables():
        square = hsq[...]
        high, low = split(square[0:GRID_PAD])
        hk[:, 0:LANES] = high
        hk[:, LANES:] = low
        turned = square.T[0:ROWS]
        lebedev = jnp.broadcast_to(leb_ref[...], (ROWS, GRID))
        hsq[0:ROWS, :] = jnp.zeros((ROWS, LANES), F32)
        return turned, lebedev

    turned, lebedev = project_tables()
    lebw = jnp.concatenate([lebedev, jnp.zeros((ROWS, GRID_K - GRID), F32)], axis=1)
    weighted = turned * lebw
    high, low = split(weighted)
    ht[0:ROWS, :] = high
    ht[ROWS:, :] = low
    rowk = lax.broadcasted_iota(jnp.int32, (8, GRID_K), 0)
    three = jnp.where(rowk < 3, pltpu.roll(weighted[0:8], 7, 0), 0.0)
    high3 = three.astype(BF16).astype(F32)
    htm[...] = jnp.concatenate([high3, three - high3], axis=0).astype(BF16)

    live = jnp.where(lax.broadcasted_iota(jnp.int32, (1, LANES), 1) < counts_ref[0, 0], 1.0, 0.0)
    degrees = degree_rows(ROWS)
    gain = live * (2.0 * degrees + 1.0) / (4.0 * math.pi)
    degrees = degrees[0:CROWS]

    column = columns(cidx_ref[...], me, plan)
    weight = cw_ref[...]
    dist = cd_ref[...]
    sin_t = jnp.sin(ct_ref[...])
    phi = cp_ref[...]
    colb[0:PAIRS, :] = column
    values = (
        weight,
        jnp.log(RADIUS_SCALE / dist),
        weight / (dist * dist * dist),
        sin_t * jnp.cos(phi),
        sin_t * jnp.sin(phi),
        jnp.cos(ct_ref[...]),
    )
    for v, value in enumerate(values):
        pk[v, 0:PAIRS, :] = value

    def packed_of(load):
        out = load(0)
        for j in range(1, GROUPS):
            out = jnp.where(group8 == j, rolled(load(GROUPS * j), BORDER * j), out)
        return out

    column_p = packed_of(lambda r: colb[r:r + 8, :])
    value_p = [packed_of(lambda r, v=v: pk[v, r:r + 8, :]) for v in range(len(values))]

    in_own = (column >= 0) & (column < LANES)
    weight_own = jnp.where(in_own, weight, 0.0)
    lanes_own = column & (LANES - 1)
    weight_rem = jnp.where(column_p >= LANES, value_p[0], 0.0)
    lanes_rem = column_p & (LANES - 1)
    tile_rem = column_p >> 7

    def spread(row, rows):
        return jnp.broadcast_to(row, (rows, LANES))

    row128 = lax.broadcasted_iota(jnp.int32, (LANES, LANES), 0)
    for k in range(PAIRS):
        wr[k] = jnp.exp(degrees * spread(values[1][k:k + 1], CROWS)) * spread(weight_own[k:k + 1], CROWS)
        ohown[:, k * LANES:(k + 1) * LANES] = jnp.where(row128 == spread(column[k:k + 1], LANES), 1.0, 0.0).astype(BF16)
        for c in range(3):
            edir[k, c:c + 1, :] = values[3 + c][k:k + 1]
    for g in range(GROUPS):
        wrp[g] = jnp.exp(degrees * spread(value_p[1][g:g + 1], CROWS)) * spread(weight_rem[g:g + 1], CROWS)
        for t in range(plan.tiles):
            ohrem[t * LANES:(t + 1) * LANES, g * LANES:(g + 1) * LANES] = jnp.where(
                row128 + (t + 1) * LANES == spread(column_p[g:g + 1], LANES), 1.0, 0.0
            ).astype(BF16)
        for c in range(3):
            edirp[g, c:c + 1, :] = value_p[3 + c][g:g + 1]

    tcol = columns(tidx_ref[...], me, plan)
    cubed = td_ref[...] * td_ref[...] * td_ref[...]
    screen = jnp.exp(-THOLE_DAMPING * cubed)
    scaled = tw_ref[...] / cubed
    lam3 = scaled * (1.0 - screen)
    lam5 = 3.0 * scaled * (1.0 - (1.0 + THOLE_DAMPING * cubed) * screen)
    tsin = jnp.sin(tt_ref[...])
    for v, value in enumerate((
        tsin * jnp.cos(tp_ref[...]), tsin * jnp.sin(tp_ref[...]), jnp.cos(tt_ref[...]), lam3, lam5,
    )):
        thc[v] = value
    tlanes = tcol & (LANES - 1)
    ttile = tcol >> 7

    def moment_fields(s):
        put_columns(cs[...])
        out = jnp.dot(htm[...], point_values(), preferred_element_type=F32)
        moment = out[0:8, 0:LANES] + out[0:8, LANES:] + out[8:, 0:LANES]
        packed = jnp.where(group8 == 0, moment, 0.0)
        wide = packed
        for j in range(1, GROUPS):
            wide = wide + rolled(packed, BORDER * j)

        def field(e, strength, m):
            along = jnp.sum(e * m, axis=0, keepdims=True)
            f = strength * (3.0 * e * along - m)
            high = f.astype(BF16).astype(F32)
            return jnp.concatenate([high, f - high], axis=0).astype(BF16)

        for k in range(PAIRS):
            fown[:, k * LANES:(k + 1) * LANES] = field(edir[k], values[2][k:k + 1], moment)
        for g in range(GROUPS):
            frem[:, g * LANES:(g + 1) * LANES] = field(edirp[g], value_p[2][g:g + 1], wide)
        turn = (((1,), (1,)), ((), ()))
        away = lax.dot_general(frem[...], ohrem[...], turn, preferred_element_type=F32)
        dip_rows = pltpu.roll(ds[...], 3, 0)
        for t in range(plan.tiles):
            part = away[:, t * LANES:(t + 1) * LANES]
            fdbuf[s, t] = jnp.where(iota8 < 3, part[0:8] + part[8:], dip_rows)
        each(f_copy, s, lambda c: c.start())
        mine = lax.dot_general(fown[...], ohown[...], turn, preferred_element_type=F32)
        return mine[0:8] + mine[8:]

    def put_columns(z):
        high, low = split(z)
        for base in (0, LANES):
            zs[base:base + ROWS, 0:LANES] = high
            zs[base:base + ROWS, LANES:] = low

    def point_values():
        out = jnp.dot(hk[...], zs[...], preferred_element_type=F32)
        high, low = split((out[:, 0:LANES] + out[:, LANES:]) * ind[...])
        ws[0:GRID_PAD, 0:LANES] = high
        ws[0:GRID_PAD, LANES:] = low
        return ws[...]

    for s in range(ITERS):
        own_field = moment_fields(s)

        table = cs[0:CROWS, :]
        coupled = jnp.zeros((CROWS, LANES), F32)
        for k in range(PAIRS):
            coupled = coupled + wr[k] * lane_take(table, spread(lanes_own[k:k + 1], CROWS))
        arrive(c_copy, s)
        for t in range(plan.tiles):
            for j in range(GROUPS):
                block = jnp.zeros((PACK, LANES), F32)
                for m in range(GROUPS):
                    slot = GROUPS * t + m
                    if slot >= plan.count or slot == plan.own:
                        continue
                    block = jnp.where(group24 == m, rolled(cbuf[s, slot], BORDER * (m - j)), block)
                pool[t, j * PACK:(j + 1) * PACK, :] = block
        far = jnp.zeros((CROWS, LANES), F32)
        for g in range(GROUPS):
            lanes = spread(lanes_rem[g:g + 1], CROWS)
            tiles = spread(tile_rem[g:g + 1], CROWS)
            got = lane_take(pool[0, 0:CROWS, :], lanes)
            for t in range(1, plan.tiles):
                got = jnp.where(tiles == t + 1, lane_take(pool[t, 0:CROWS, :], lanes), got)
            far = far + wrp[g] * got
        far = far + rolled(far, 64)
        far = far + rolled(far, 32)
        coupled = coupled + jnp.where(lane_group((CROWS, LANES)) == 0, far, 0.0)

        put_columns(jnp.concatenate([coupled, zero8], axis=0))
        inj[1:4, :] = INJECT_SCALE * ds[0:3, :]
        out = jnp.dot(ht[...], point_values(), preferred_element_type=F32)
        projected = out[0:ROWS, 0:LANES] + out[0:ROWS, LANES:] + out[ROWS:, 0:LANES]
        fresh = gain * (src[...] + inj[...] - projected)
        if s < ITERS - 1:
            cs[...] = fresh
            pack_coefs(s + 1)
            each(c_copy, s + 1, lambda c: c.start())
        else:
            coef_out[...] = fresh[0:COEF]

        arrive(f_copy, s)
        reaction = own_field
        for m in range(GROUPS):
            total = None
            for slot in plan.others:
                if plan.mirror(slot) % GROUPS == m:
                    total = fdrecv[s, slot] if total is None else total + fdrecv[s, slot]
            if total is not None:
                reaction = reaction + jnp.where(group8 == 0, rolled(total, -BORDER * m), 0.0)
        tables = [pltpu.roll(ds[...], 3, 0)]
        for t in range(plan.tiles):
            block = zero8
            for m in range(GROUPS):
                slot = GROUPS * t + m
                if slot >= plan.count or slot == plan.own:
                    continue
                block = jnp.where(group8 == m, rolled(fdrecv[s, slot], BORDER * m), block)
            tables.append(block)
        partner = []
        for c in range(3):
            got = jnp.zeros((PAIRS, LANES), F32)
            for t, block in enumerate(tables):
                got = jnp.where(ttile == t, lane_take(spread(block[3 + c:4 + c], PAIRS), tlanes), got)
            partner.append(got)
        along = thc[4] * (thc[0] * partner[0] + thc[1] * partner[1] + thc[2] * partner[2])
        for c in range(3):
            tmp[c:c + 1, :] = jnp.sum(thc[c] * along - thc[3] * partner[c], axis=0, keepdims=True)
        moved = live * polar_ref[...] * (ext[...] + tmp[...] + reaction)
        moved = jnp.where(iota8 < 3, moved, 0.0)
        if s < ITERS - 1:
            ds[...] = moved
        else:
            dip_out[...] = moved[0:3]

    for s in range(ITERS):
        each(c_copy, s, lambda c: c.wait_send())
        each(f_copy, s, lambda c: c.wait_send())


def rows_of(x):
    return x.reshape(x.shape[0], x.shape[-1])


def local(plan, *args):
    (coef, dip, source, ind, polar, ext, counts, cidx, cw, cd, ct, cp,
     tidx, tw, td, tt, tp, harm, leb) = args
    flat = [rows_of(x) for x in (coef, dip, source, ind)]
    flat += [polar.reshape(1, LANES), rows_of(ext), counts.reshape(1, 1)]
    flat += [rows_of(x) for x in (cidx, cw, cd, ct, cp, tidx, tw, td, tt, tp)]
    flat += [harm, leb.reshape(1, GRID)]
    vmem = pl.BlockSpec(memory_space=pltpu.VMEM)
    smem = pl.BlockSpec(memory_space=pltpu.SMEM)
    scratch = [
        ((ROWS, LANES), F32), ((8, LANES), F32), ((ROWS, LANES), F32), ((ROWS, LANES), F32),
        ((8, LANES), F32), ((8, LANES), F32),
        ((ITERS, PACK, LANES), F32), ((ITERS, plan.count, PACK, LANES), F32),
        ((ITERS, plan.tiles, 8, LANES), F32), ((ITERS, plan.count, 8, LANES), F32),
        ((24, LANES), jnp.int32), ((6, 24, LANES), F32),
        ((PAIRS, CROWS, LANES), F32), ((GROUPS, CROWS, LANES), F32),
        ((PAIRS, 8, LANES), F32), ((GROUPS, 8, LANES), F32), ((8, LANES), F32),
        ((LANES, PAIRS * LANES), BF16), ((plan.tiles * LANES, GROUPS * LANES), BF16),
        ((16, PAIRS * LANES), BF16), ((16, GROUPS * LANES), BF16),
        ((GRID_PAD, 2 * LANES), BF16), ((2 * ROWS, GRID_K), BF16), ((16, GRID_K), BF16),
        ((GRID_K, LANES), F32),
        ((2 * LANES, 2 * LANES), BF16), ((GRID_K, 2 * LANES), BF16), ((GRID_PAD, LANES), F32),
        ((5, PAIRS, LANES), F32), ((plan.tiles, ROWS, LANES), F32),
    ]
    semaphores = [pltpu.SemaphoreType.DMA((ITERS, plan.count))] * 4
    coef_new, dip_new = pl.pallas_call(
        functools.partial(kernel, plan),
        out_shape=(jax.ShapeDtypeStruct((COEF, LANES), F32), jax.ShapeDtypeStruct((3, LANES), F32)),
        in_specs=[smem if i == 6 else vmem for i in range(len(flat))],
        out_specs=(vmem, vmem),
        scratch_shapes=[pltpu.VMEM(shape, kind) for shape, kind in scratch] + semaphores,
        compiler_params=pltpu.CompilerParams(
            collective_id=0, has_side_effects=True, vmem_limit_bytes=32 * 1024 * 1024
        ),
    )(*flat)
    return coef_new.reshape(coef.shape), dip_new.reshape(dip.shape)


def solution(mesh):
    plan = Slots(tuple(mesh.shape[a] for a in AXES))
    lead = P(None, ("grp", "gx"), "gy", "gz", None)
    flat = P(("grp", "gx"), "gy", "gz", None)
    in_specs = (lead,) * 4 + (flat, lead, P(("grp", "gx"), "gy", "gz")) + (lead,) * 10 + (P(), P())
    return jax.shard_map(
        functools.partial(local, plan), mesh=mesh, in_specs=in_specs, out_specs=(lead, lead), check_vma=False
    )
```

```python
import functools
import itertools
import math

import jax
import jax.numpy as jnp
from jax import lax
from jax.experimental import pallas as pl
from jax.experimental.pallas import tpu as pltpu
from jax.sharding import PartitionSpec as P

ITERS = 3
AXES = ("gx", "gy", "gz")
MESH = pl.DeviceIdType.MESH
THOLE_DAMPING = 0.39
INJECT_SCALE = 2.0
RADIUS_SCALE = 0.9

COEF = 81
GRID = 302
LANES = 128
BORDER = 32
PAIRS = 16
GROUPS = LANES // BORDER
PACK = 24
ROWS = GROUPS * PACK
CROWS = 88
GRID_PAD = 304
GRID_K = 384
F32 = jnp.float32
BF16 = jnp.bfloat16
OPERANDS = (
    "coef", "dip", "source", "ind", "cidx", "cw", "cd", "ct", "cp",
    "tidx", "tw", "td", "tt", "tp", "ext", "polar", "harm", "leb", "counts",
)


def axis_digits(size):
    if size >= 3:
        return (-1, 0, 1)
    return (0, 1) if size == 2 else (0,)


class Slots:
    def __init__(self, sizes):
        self.sizes = sizes
        self.digits = [axis_digits(n) for n in sizes]
        self.all = list(itertools.product(*[range(len(d)) for d in self.digits]))
        self.count = len(self.all)
        self.tiles = -(-self.count // GROUPS)
        centre = tuple(d.index(0) for d in self.digits)
        self.own = self.all.index(centre)
        self.others = [i for i in range(self.count) if i != self.own]
        self.others.sort(key=lambda i: -sum(a != b for a, b in zip(self.all[i][:2], centre[:2])))

    def mirror(self, slot):
        place = self.all[slot]
        back = tuple(2 - e if n >= 3 else e for e, n in zip(place, self.sizes))
        return self.all.index(back)

    def device(self, slot, me):
        ids = {}
        for axis, n, d, e, i in zip(AXES, self.sizes, self.digits, self.all[slot], me):
            if d[e] == 0:
                continue
            ids[axis] = i + d[e] if n >= 3 else 1 - i
        return ids

    def valid(self, slot, me):
        cond = None
        for n, d, e, i in zip(self.sizes, self.digits, self.all[slot], me):
            if n < 3 or d[e] == 0:
                continue
            here = (i + d[e] >= 0) & (i + d[e] < n)
            cond = here if cond is None else cond & here
        return cond


def when(cond, fn):
    if cond is None:
        fn()
    else:
        pl.when(cond)(fn)


def lane_group(shape):
    return lax.broadcasted_iota(jnp.int32, shape, len(shape) - 1) >> 5


def lane_take(table, lanes):
    return jnp.take_along_axis(table, lanes, axis=1, mode="promise_in_bounds")


def rolled(x, shift):
    shift = shift % LANES
    return x if shift == 0 else pltpu.roll(x, shift, 1)


def degree_rows(rows):
    row = lax.broadcasted_iota(jnp.int32, (rows, LANES), 0)
    total = jnp.zeros((rows, LANES), F32)
    for level in range(1, math.isqrt(COEF)):
        total = total + jnp.where(row >= level * level, 1.0, 0.0)
    return total


def sine_cosine(angle):
    def sine(y):
        z = y * y
        total = jnp.full_like(y, 1.0 / math.factorial(13))
        for n in (11, 9, 7, 5, 3, 1):
            total = total * z + (-1.0) ** (n // 2) / math.factorial(n)
        return total * y

    quarter = math.pi / 2 - jnp.abs(angle)
    up = sine(math.pi / 2 - jnp.abs(quarter))
    return jnp.where(angle < 0.0, -up, up), sine(quarter)


def split(x):
    high = x.astype(BF16)
    return high, (x - high.astype(F32)).astype(BF16)


def columns(index, me, plan):
    block = index >> 5
    within = index & 31
    bx = (block * 57) >> 9
    rest = block - 9 * bx
    by = (rest * 171) >> 9
    bz = rest - 3 * by
    inside = None
    slot = jnp.zeros_like(index)
    for n, d, b, i in zip(plan.sizes, plan.digits, (bx, by, bz), me):
        step = b - 1
        here = (step + i >= 0) & (step + i < n)
        inside = here if inside is None else inside & here
        digit = b if n >= 3 else step * step
        slot = slot * len(d) + (digit if n >= 2 else jnp.zeros_like(index))
    remote = jnp.where(inside, LANES + slot * BORDER + within, -1)
    column = jnp.where(block == 13, within, remote)
    return jnp.where(index >= 27 * BORDER, index - 27 * BORDER, column)


def kernel(
    plan,
    *refs,
):
    count = len(OPERANDS)
    given = refs[:count]
    coef_out, dip_out = refs[count:count + 2]
    held = dict(zip(OPERANDS, refs[count + 2:2 * count + 2]))
    loads = {
        name: pltpu.make_async_copy(there, held[name], refs[-1].at[i])
        for i, (name, there) in enumerate(zip(OPERANDS, given))
    }
    body(plan, loads, held, coef_out, dip_out, *refs[2 * count + 2:-1])


def body(
    plan, loads, held, coef_out, dip_out,
    cs, ds, src, inj, ext, tmp, sbuf, cbuf, fdbuf, fdrecv,
    colb, pk, wr, wrp, edir, edirp, stren, ohown, ohrem, fown, frem,
    hk, ht, htm, hsq, leb, zs, ws, ind, thc, pool,
    csend, crecv, fsend, frecv,
):
    def got(name):
        loads[name].wait()
        ref = held[name]
        return ref[:, 0, :] if len(ref.shape) == 3 else ref[...]

    me = tuple(lax.axis_index(a) for a in AXES)
    barrier = pltpu.get_barrier_semaphore()
    number = 0
    for slot in plan.others:
        cond = plan.valid(slot, me)
        ids = plan.device(slot, me)
        when(cond, lambda ids=ids: pl.semaphore_signal(barrier, inc=1, device_id=ids, device_id_type=MESH))
        number = number + (1 if cond is None else cond.astype(jnp.int32))

    for name in OPERANDS:
        loads[name].start()
    group24 = lane_group((PACK, LANES))
    group8 = lane_group((8, LANES))
    iota8 = lax.broadcasted_iota(jnp.int32, (8, LANES), 0)

    cs[...] = jnp.zeros_like(cs)
    ds[...] = jnp.zeros_like(ds)
    for slot in plan.others:
        cond = plan.valid(slot, me)
        if cond is not None:
            def clear(slot=slot):
                for s in range(ITERS):
                    cbuf[s, slot] = jnp.zeros((PACK, LANES), F32)
                    fdrecv[s, slot] = jnp.zeros((8, LANES), F32)
            pl.when(jnp.logical_not(cond))(clear)

    def copy(bufs, s, slot, place):
        src, dst, send, recv = bufs
        return pltpu.make_async_remote_copy(
            src_ref=src(s, slot), dst_ref=dst.at[s, place],
            send_sem=send.at[s, slot], recv_sem=recv.at[s, place],
            device_id=plan.device(slot, me), device_id_type=MESH,
        )

    c_bufs = (lambda s, slot: sbuf.at[s], cbuf, csend, crecv)
    f_bufs = (lambda s, slot: fdbuf.at[s, slot // GROUPS], fdrecv, fsend, frecv)

    def start(bufs, s):
        for slot in plan.others:
            when(plan.valid(slot, me), lambda slot=slot: copy(bufs, s, slot, plan.mirror(slot)).start())

    def arrive(bufs, s):
        for slot in reversed(plan.others):
            when(plan.valid(slot, me), lambda slot=slot: copy(bufs, s, slot, slot).wait_recv())

    def sent(bufs, s):
        for slot in plan.others:
            when(plan.valid(slot, me), lambda slot=slot: copy(bufs, s, slot, plan.mirror(slot)).wait_send())

    def pack_coefs(s):
        packed = cs[0:PACK, :]
        for j in range(1, GROUPS):
            packed = jnp.where(group24 == j, rolled(cs[j * PACK:(j + 1) * PACK, :], BORDER * j), packed)
        sbuf[s] = packed

    cs[0:COEF, :] = got("coef")
    pack_coefs(0)

    zero8 = jnp.zeros((8, LANES), F32)
    src[...] = jnp.zeros_like(src)
    src[0:COEF, :] = got("source")
    ds[0:3, :] = got("dip")
    inj[...] = jnp.zeros_like(inj)
    ext[...] = zero8
    ext[0:3, :] = got("ext")
    tmp[...] = zero8
    ind[...] = jnp.zeros_like(ind)
    ind[0:GRID, :] = got("ind")
    zs[...] = jnp.zeros_like(zs)
    ws[...] = jnp.zeros_like(ws)
    hsq[...] = jnp.zeros_like(hsq)
    hsq[0:COEF, 0:GRID] = got("harm")
    pk[...] = jnp.zeros_like(pk)
    colb[...] = jnp.zeros_like(colb)
    edir[...] = jnp.zeros_like(edir)
    edirp[...] = jnp.zeros_like(edirp)
    stren[...] = jnp.zeros_like(stren)

    square = hsq[...]
    high, low = split(square.T[0:GRID_PAD])
    hk[:, 0:LANES] = high
    hk[:, LANES:] = low
    leb[...] = jnp.zeros_like(leb)
    leb[0:1, 0:GRID] = got("leb").reshape(1, GRID)
    weighted = square[0:ROWS] * jnp.broadcast_to(leb[0:1, :], (ROWS, GRID_K))
    high, low = split(weighted)
    ht[0:ROWS, :] = high
    ht[ROWS:, :] = low
    rowk = lax.broadcasted_iota(jnp.int32, (8, GRID_K), 0)
    three = jnp.where(rowk < 3, pltpu.roll(weighted[0:8], 7, 0), 0.0)
    high3 = three.astype(BF16).astype(F32)
    htm[...] = jnp.concatenate([high3, three - high3], axis=0).astype(BF16)

    live = jnp.where(lax.broadcasted_iota(jnp.int32, (1, LANES), 1) < jnp.broadcast_to(got("counts"), (1, LANES)), 1.0, 0.0)
    degrees = degree_rows(ROWS)
    gain = live * (2.0 * degrees + 1.0) / (4.0 * math.pi)
    degrees = degrees[0:CROWS]

    column = columns(got("cidx"), me, plan)
    weight = got("cw")
    dist = got("cd")
    sin_t, cos_t = sine_cosine(got("ct"))
    sin_p, cos_p = sine_cosine(got("cp"))
    colb[0:PAIRS, :] = column
    values = (
        weight,
        jnp.log(RADIUS_SCALE / dist),
        weight / (dist * dist * dist),
        sin_t * cos_p,
        sin_t * sin_p,
        cos_t,
    )
    for v, value in enumerate(values):
        pk[v, 0:PAIRS, :] = value

    def packed_of(load):
        out = load(0)
        for j in range(1, GROUPS):
            out = jnp.where(group8 == j, rolled(load(GROUPS * j), BORDER * j), out)
        return out

    column_p = packed_of(lambda r: colb[r:r + 8, :])
    value_p = [packed_of(lambda r, v=v: pk[v, r:r + 8, :]) for v in range(len(values))]

    in_own = (column >= 0) & (column < LANES)
    weight_own = jnp.where(in_own, weight, 0.0)
    lanes_own = column & (LANES - 1)
    weight_rem = jnp.where(column_p >= LANES, value_p[0], 0.0)
    lanes_rem = column_p & (LANES - 1)
    tile_rem = column_p >> 7

    def spread(row, rows):
        return jnp.broadcast_to(row, (rows, LANES))

    pl.semaphore_wait(barrier, number)
    start(c_bufs, 0)

    row128 = lax.broadcasted_iota(jnp.int32, (LANES, LANES), 0)
    for k in range(PAIRS):
        wr[k] = jnp.exp(degrees * spread(values[1][k:k + 1], CROWS)) * spread(weight_own[k:k + 1], CROWS)
        ohown[:, k * LANES:(k + 1) * LANES] = jnp.where(row128 == spread(column[k:k + 1], LANES), 1.0, 0.0).astype(BF16)
        for c in range(3):
            edir[k, c:c + 1, :] = values[3 + c][k:k + 1]
    for g in range(GROUPS):
        wrp[g] = jnp.exp(degrees * spread(value_p[1][g:g + 1], CROWS)) * spread(weight_rem[g:g + 1], CROWS)
        for t in range(plan.tiles):
            ohrem[t * LANES:(t + 1) * LANES, g * LANES:(g + 1) * LANES] = jnp.where(
                row128 + (t + 1) * LANES == spread(column_p[g:g + 1], LANES), 1.0, 0.0
            ).astype(BF16)
        for c in range(3):
            edirp[g, c:c + 1, :] = value_p[3 + c][g:g + 1]

    tcol = columns(got("tidx"), me, plan)
    apart = got("td")
    cubed = apart * apart * apart
    screen = jnp.exp(-THOLE_DAMPING * cubed)
    scaled = got("tw") / cubed
    lam3 = scaled * (1.0 - screen)
    lam5 = 3.0 * scaled * (1.0 - (1.0 + THOLE_DAMPING * cubed) * screen)
    sin_t, cos_t = sine_cosine(got("tt"))
    sin_p, cos_p = sine_cosine(got("tp"))
    polar = live * got("polar")
    for v, value in enumerate((
        sin_t * cos_p, sin_t * sin_p, cos_t, lam3, lam5,
    )):
        thc[v] = value
    tlanes = tcol & (LANES - 1)
    ttile = tcol >> 7

    def moment_fields(s):
        put_columns(cs[...])
        out = jnp.dot(htm[...], point_values(), preferred_element_type=F32)
        moment = out[0:8, 0:LANES] + out[0:8, LANES:] + out[8:, 0:LANES]
        packed = jnp.where(group8 == 0, moment, 0.0)
        wide = packed
        for j in range(1, GROUPS):
            wide = wide + rolled(packed, BORDER * j)

        def field(e, strength, m):
            along = jnp.sum(e * m, axis=0, keepdims=True)
            f = strength * (3.0 * e * along - m)
            high = f.astype(BF16).astype(F32)
            return jnp.concatenate([high, f - high], axis=0).astype(BF16)

        for k in range(PAIRS):
            fown[:, k * LANES:(k + 1) * LANES] = field(edir[k], values[2][k:k + 1], moment)
        for g in range(GROUPS):
            frem[:, g * LANES:(g + 1) * LANES] = field(edirp[g], value_p[2][g:g + 1], wide)
        turn = (((1,), (1,)), ((), ()))
        away = lax.dot_general(frem[...], ohrem[...], turn, preferred_element_type=F32)
        dip_rows = pltpu.roll(ds[...], 3, 0)
        for t in range(plan.tiles):
            part = away[:, t * LANES:(t + 1) * LANES]
            fdbuf[s, t] = jnp.where(iota8 < 3, part[0:8] + part[8:], dip_rows)
        start(f_bufs, s)
        mine = lax.dot_general(fown[...], ohown[...], turn, preferred_element_type=F32)
        return mine[0:8] + mine[8:]

    def put_columns(z):
        high, low = split(z)
        for base in (0, LANES):
            zs[base:base + ROWS, 0:LANES] = high
            zs[base:base + ROWS, LANES:] = low

    def point_values():
        out = jnp.dot(hk[...], zs[...], preferred_element_type=F32)
        high, low = split((out[:, 0:LANES] + out[:, LANES:]) * ind[...])
        ws[0:GRID_PAD, 0:LANES] = high
        ws[0:GRID_PAD, LANES:] = low
        return ws[...]

    for s in range(ITERS):
        own_field = moment_fields(s)

        table = cs[0:CROWS, :]
        coupled = jnp.zeros((CROWS, LANES), F32)
        for k in range(PAIRS):
            coupled = coupled + wr[k] * lane_take(table, spread(lanes_own[k:k + 1], CROWS))
        arrive(c_bufs, s)
        for t in range(plan.tiles):
            for j in range(GROUPS):
                block = jnp.zeros((PACK, LANES), F32)
                for m in range(GROUPS):
                    slot = GROUPS * t + m
                    if slot >= plan.count or slot == plan.own:
                        continue
                    block = jnp.where(group24 == m, rolled(cbuf[s, slot], BORDER * (m - j)), block)
                pool[t, j * PACK:(j + 1) * PACK, :] = block
        far = jnp.zeros((CROWS, LANES), F32)
        for g in range(GROUPS):
            lanes = spread(lanes_rem[g:g + 1], CROWS)
            tiles = spread(tile_rem[g:g + 1], CROWS)
            found = lane_take(pool[0, 0:CROWS, :], lanes)
            for t in range(1, plan.tiles):
                found = jnp.where(tiles == t + 1, lane_take(pool[t, 0:CROWS, :], lanes), found)
            far = far + wrp[g] * found
        far = far + rolled(far, 64)
        far = far + rolled(far, 32)
        coupled = coupled + jnp.where(lane_group((CROWS, LANES)) == 0, far, 0.0)

        put_columns(jnp.concatenate([coupled, zero8], axis=0))
        inj[1:4, :] = INJECT_SCALE * ds[0:3, :]
        out = jnp.dot(ht[...], point_values(), preferred_element_type=F32)
        projected = out[0:ROWS, 0:LANES] + out[0:ROWS, LANES:] + out[ROWS:, 0:LANES]
        fresh = gain * (src[...] + inj[...] - projected)
        if s < ITERS - 1:
            cs[...] = fresh
            pack_coefs(s + 1)
            start(c_bufs, s + 1)
        else:
            coef_out[:, 0, :] = fresh[0:COEF]

        arrive(f_bufs, s)
        reaction = own_field
        for m in range(GROUPS):
            total = None
            for slot in plan.others:
                if plan.mirror(slot) % GROUPS == m:
                    total = fdrecv[s, slot] if total is None else total + fdrecv[s, slot]
            if total is not None:
                reaction = reaction + jnp.where(group8 == 0, rolled(total, -BORDER * m), 0.0)
        tables = [pltpu.roll(ds[...], 3, 0)]
        for t in range(plan.tiles):
            block = zero8
            for m in range(GROUPS):
                slot = GROUPS * t + m
                if slot >= plan.count or slot == plan.own:
                    continue
                block = jnp.where(group8 == m, rolled(fdrecv[s, slot], BORDER * m), block)
            tables.append(block)
        partner = []
        for c in range(3):
            found = jnp.zeros((PAIRS, LANES), F32)
            for t, block in enumerate(tables):
                found = jnp.where(ttile == t, lane_take(spread(block[3 + c:4 + c], PAIRS), tlanes), found)
            partner.append(found)
        along = thc[4] * (thc[0] * partner[0] + thc[1] * partner[1] + thc[2] * partner[2])
        for c in range(3):
            tmp[c:c + 1, :] = jnp.sum(thc[c] * along - thc[3] * partner[c], axis=0, keepdims=True)
        moved = polar * (ext[...] + tmp[...] + reaction)
        moved = jnp.where(iota8 < 3, moved, 0.0)
        if s < ITERS - 1:
            ds[...] = moved
        else:
            dip_out[:, 0, :] = moved[0:3]

    for s in range(ITERS):
        sent(c_bufs, s)
        sent(f_bufs, s)


def rows_of(x):
    shape = (x.shape[0], x.shape[-1]) if x.shape[0] % 8 == 0 else (x.shape[0], 1, x.shape[-1])
    return x.reshape(shape)


def local(plan, *args):
    (coef, dip, source, ind, polar, ext, counts, cidx, cw, cd, ct, cp,
     tidx, tw, td, tt, tp, harm, leb) = args
    flat = [rows_of(x) for x in (coef, dip, source, ind, cidx, cw, cd, ct, cp, tidx, tw, td, tt, tp, ext)]
    flat += [polar.reshape(1, LANES), harm.T, leb, counts]
    vmem = pl.BlockSpec(memory_space=pltpu.VMEM)
    held = [pltpu.VMEM(x.shape, x.dtype) for x in flat]
    scratch = [
        ((ROWS, LANES), F32), ((8, LANES), F32), ((ROWS, LANES), F32), ((ROWS, LANES), F32),
        ((8, LANES), F32), ((8, LANES), F32),
        ((ITERS, PACK, LANES), F32), ((ITERS, plan.count, PACK, LANES), F32),
        ((ITERS, plan.tiles, 8, LANES), F32), ((ITERS, plan.count, 8, LANES), F32),
        ((24, LANES), jnp.int32), ((6, 24, LANES), F32),
        ((PAIRS, CROWS, LANES), F32), ((GROUPS, CROWS, LANES), F32),
        ((PAIRS, 8, LANES), F32), ((GROUPS, 8, LANES), F32), ((8, LANES), F32),
        ((LANES, PAIRS * LANES), BF16), ((plan.tiles * LANES, GROUPS * LANES), BF16),
        ((16, PAIRS * LANES), BF16), ((16, GROUPS * LANES), BF16),
        ((GRID_PAD, 2 * LANES), BF16), ((2 * ROWS, GRID_K), BF16), ((16, GRID_K), BF16),
        ((LANES, GRID_K), F32), ((8, GRID_K), F32),
        ((2 * LANES, 2 * LANES), BF16), ((GRID_K, 2 * LANES), BF16), ((GRID_PAD, LANES), F32),
        ((5, PAIRS, LANES), F32), ((plan.tiles, ROWS, LANES), F32),
    ]
    semaphores = [pltpu.SemaphoreType.DMA((ITERS, plan.count))] * 4 + [pltpu.SemaphoreType.DMA((len(flat),))]
    coef_new, dip_new = pl.pallas_call(
        functools.partial(kernel, plan),
        out_shape=(jax.ShapeDtypeStruct((COEF, 1, LANES), F32), jax.ShapeDtypeStruct((3, 1, LANES), F32)),
        in_specs=[pl.BlockSpec(memory_space=pltpu.HBM)] * len(flat),
        out_specs=(vmem, vmem),
        scratch_shapes=held + [pltpu.VMEM(shape, kind) for shape, kind in scratch] + semaphores,
        compiler_params=pltpu.CompilerParams(
            collective_id=0, has_side_effects=True, vmem_limit_bytes=60 * 1024 * 1024
        ),
    )(*flat)
    return coef_new.reshape(coef.shape), dip_new.reshape(dip.shape)


def solution(mesh):
    plan = Slots(tuple(mesh.shape[a] for a in AXES))
    lead = P(None, ("grp", "gx"), "gy", "gz", None)
    flat = P(("grp", "gx"), "gy", "gz", None)
    in_specs = (lead,) * 4 + (flat, lead, P(("grp", "gx"), "gy", "gz")) + (lead,) * 10 + (P(), P())
    return jax.shard_map(
        functools.partial(local, plan), mesh=mesh, in_specs=in_specs, out_specs=(lead, lead), check_vma=False
    )
```

```python
import functools
import itertools
import math

import jax
import jax.numpy as jnp
from jax import lax
from jax.experimental import pallas as pl
from jax.experimental.pallas import tpu as pltpu
from jax.sharding import PartitionSpec as P

ITERS = 3
AXES = ("gx", "gy", "gz")
MESH = pl.DeviceIdType.MESH
THOLE_DAMPING = 0.39
INJECT_SCALE = 2.0
RADIUS_SCALE = 0.9

COEF = 81
GRID = 302
LANES = 128
BORDER = 32
PAIRS = 16
GROUPS = LANES // BORDER
PACK = 24
ROWS = GROUPS * PACK
CROWS = 88
GRID_PAD = 304
GRID_K = 384
F32 = jnp.float32
BF16 = jnp.bfloat16
OPERANDS = (
    "coef", "dip", "source", "ind", "cidx", "cw", "cd", "ct", "cp",
    "tidx", "tw", "td", "tt", "tp", "ext", "polar", "harm", "leb", "counts",
)


def axis_digits(size):
    if size >= 3:
        return (-1, 0, 1)
    return (0, 1) if size == 2 else (0,)


class Slots:
    def __init__(self, sizes):
        self.sizes = sizes
        self.digits = [axis_digits(n) for n in sizes]
        self.all = list(itertools.product(*[range(len(d)) for d in self.digits]))
        self.count = len(self.all)
        self.tiles = -(-self.count // GROUPS)
        centre = tuple(d.index(0) for d in self.digits)
        self.own = self.all.index(centre)
        self.others = [i for i in range(self.count) if i != self.own]
        self.others.sort(key=lambda i: -sum(a != b for a, b in zip(self.all[i][:2], centre[:2])))

    def mirror(self, slot):
        place = self.all[slot]
        back = tuple(2 - e if n >= 3 else e for e, n in zip(place, self.sizes))
        return self.all.index(back)

    def device(self, slot, me):
        ids = {}
        for axis, n, d, e, i in zip(AXES, self.sizes, self.digits, self.all[slot], me):
            if d[e] == 0:
                continue
            ids[axis] = i + d[e] if n >= 3 else 1 - i
        return ids

    def valid(self, slot, me):
        cond = None
        for n, d, e, i in zip(self.sizes, self.digits, self.all[slot], me):
            if n < 3 or d[e] == 0:
                continue
            here = (i + d[e] >= 0) & (i + d[e] < n)
            cond = here if cond is None else cond & here
        return cond


def when(cond, fn):
    if cond is None:
        fn()
    else:
        pl.when(cond)(fn)


def lane_group(shape):
    return lax.broadcasted_iota(jnp.int32, shape, len(shape) - 1) >> 5


def lane_take(table, lanes):
    return jnp.take_along_axis(table, lanes, axis=1, mode="promise_in_bounds")


def rolled(x, shift):
    shift = shift % LANES
    return x if shift == 0 else pltpu.roll(x, shift, 1)


def degree_rows(rows):
    row = lax.broadcasted_iota(jnp.int32, (rows, LANES), 0)
    total = jnp.zeros((rows, LANES), F32)
    for level in range(1, math.isqrt(COEF)):
        total = total + jnp.where(row >= level * level, 1.0, 0.0)
    return total


def sine_cosine(angle):
    def sine(y):
        z = y * y
        total = jnp.full_like(y, 1.0 / math.factorial(13))
        for n in (11, 9, 7, 5, 3, 1):
            total = total * z + (-1.0) ** (n // 2) / math.factorial(n)
        return total * y

    quarter = math.pi / 2 - jnp.abs(angle)
    up = sine(math.pi / 2 - jnp.abs(quarter))
    return jnp.where(angle < 0.0, -up, up), sine(quarter)


def split(x):
    high = x.astype(BF16)
    return high, (x - high.astype(F32)).astype(BF16)


def columns(index, me, plan):
    block = index >> 5
    within = index & 31
    bx = (block * 57) >> 9
    rest = block - 9 * bx
    by = (rest * 171) >> 9
    bz = rest - 3 * by
    inside = None
    slot = jnp.zeros_like(index)
    for n, d, b, i in zip(plan.sizes, plan.digits, (bx, by, bz), me):
        step = b - 1
        here = (step + i >= 0) & (step + i < n)
        inside = here if inside is None else inside & here
        digit = b if n >= 3 else step * step
        slot = slot * len(d) + (digit if n >= 2 else jnp.zeros_like(index))
    remote = jnp.where(inside, LANES + slot * BORDER + within, -1)
    column = jnp.where(block == 13, within, remote)
    return jnp.where(index >= 27 * BORDER, index - 27 * BORDER, column)


def kernel(
    plan,
    *refs,
):
    count = len(OPERANDS)
    given = refs[:count]
    coef_out, dip_out = refs[count:count + 2]
    held = dict(zip(OPERANDS, refs[count + 2:2 * count + 2]))
    loads = {
        name: pltpu.make_async_copy(there, held[name], refs[-1].at[i])
        for i, (name, there) in enumerate(zip(OPERANDS, given))
    }
    body(plan, loads, held, coef_out, dip_out, *refs[2 * count + 2:-1])


def body(
    plan, loads, held, coef_out, dip_out,
    cs, ds, src, inj, ext, tmp, sbuf, cbuf, fdbuf, fdrecv,
    colb, pk, wr, wrp, edir, edirp, stren, ohown, ohrem, fown, frem,
    hk, ht, htm, hsq, leb, zs, ws, ind, thc, pool,
    csend, crecv, fsend, frecv,
):
    def got(name):
        loads[name].wait()
        ref = held[name]
        return ref[:, 0, :] if len(ref.shape) == 3 else ref[...]

    me = tuple(lax.axis_index(a) for a in AXES)
    barrier = pltpu.get_barrier_semaphore()
    number = 0
    for slot in plan.others:
        cond = plan.valid(slot, me)
        ids = plan.device(slot, me)
        when(cond, lambda ids=ids: pl.semaphore_signal(barrier, inc=1, device_id=ids, device_id_type=MESH))
        number = number + (1 if cond is None else cond.astype(jnp.int32))

    for name in OPERANDS:
        loads[name].start()
    group24 = lane_group((PACK, LANES))
    group8 = lane_group((8, LANES))
    iota8 = lax.broadcasted_iota(jnp.int32, (8, LANES), 0)

    cs[...] = jnp.zeros_like(cs)
    ds[...] = jnp.zeros_like(ds)
    for slot in plan.others:
        cond = plan.valid(slot, me)
        if cond is not None:
            def clear(slot=slot):
                for s in range(ITERS):
                    cbuf[s, slot] = jnp.zeros((PACK, LANES), F32)
                    fdrecv[s, slot] = jnp.zeros((8, LANES), F32)
            pl.when(jnp.logical_not(cond))(clear)

    def copy(bufs, s, slot, place):
        src, dst, send, recv = bufs
        return pltpu.make_async_remote_copy(
            src_ref=src(s, slot), dst_ref=dst.at[s, place],
            send_sem=send.at[s, slot], recv_sem=recv.at[s, place],
            device_id=plan.device(slot, me), device_id_type=MESH,
        )

    c_bufs = (lambda s, slot: sbuf.at[s], cbuf, csend, crecv)
    f_bufs = (lambda s, slot: fdbuf.at[s, slot // GROUPS], fdrecv, fsend, frecv)

    def start(bufs, s):
        for slot in plan.others:
            when(plan.valid(slot, me), lambda slot=slot: copy(bufs, s, slot, plan.mirror(slot)).start())

    def arrive(bufs, s):
        for slot in reversed(plan.others):
            when(plan.valid(slot, me), lambda slot=slot: copy(bufs, s, slot, slot).wait_recv())

    def sent(bufs, s):
        for slot in plan.others:
            when(plan.valid(slot, me), lambda slot=slot: copy(bufs, s, slot, plan.mirror(slot)).wait_send())

    def pack_coefs(s):
        packed = cs[0:PACK, :]
        for j in range(1, GROUPS):
            packed = jnp.where(group24 == j, rolled(cs[j * PACK:(j + 1) * PACK, :], BORDER * j), packed)
        sbuf[s] = packed

    cs[0:COEF, :] = got("coef")
    pack_coefs(0)

    zero8 = jnp.zeros((8, LANES), F32)
    src[...] = jnp.zeros_like(src)
    src[0:COEF, :] = got("source")
    ds[0:3, :] = got("dip")
    inj[...] = jnp.zeros_like(inj)
    ext[...] = zero8
    ext[0:3, :] = got("ext")
    tmp[...] = zero8
    ind[...] = jnp.zeros_like(ind)
    ind[0:GRID, :] = got("ind")
    zs[...] = jnp.zeros_like(zs)
    ws[...] = jnp.zeros_like(ws)
    hsq[...] = jnp.zeros_like(hsq)
    hsq[0:COEF, 0:GRID] = got("harm")
    pk[...] = jnp.zeros_like(pk)
    colb[...] = jnp.zeros_like(colb)
    edir[...] = jnp.zeros_like(edir)
    edirp[...] = jnp.zeros_like(edirp)
    stren[...] = jnp.zeros_like(stren)

    square = hsq[...]
    high, low = split(square.T[0:GRID_PAD])
    hk[:, 0:LANES] = high
    hk[:, LANES:] = low
    leb[...] = jnp.zeros_like(leb)
    leb[0:1, 0:GRID] = got("leb").reshape(1, GRID)
    weighted = square[0:ROWS] * jnp.broadcast_to(leb[0:1, :], (ROWS, GRID_K))
    high, low = split(weighted)
    ht[0:ROWS, :] = high
    ht[ROWS:, :] = low
    rowk = lax.broadcasted_iota(jnp.int32, (8, GRID_K), 0)
    three = jnp.where(rowk < 3, pltpu.roll(weighted[0:8], 7, 0), 0.0)
    high3 = three.astype(BF16).astype(F32)
    htm[...] = jnp.concatenate([high3, three - high3], axis=0).astype(BF16)

    live = jnp.where(lax.broadcasted_iota(jnp.int32, (1, LANES), 1) < jnp.broadcast_to(got("counts"), (1, LANES)), 1.0, 0.0)
    degrees = degree_rows(ROWS)
    gain = live * (2.0 * degrees + 1.0) / (4.0 * math.pi)
    degrees = degrees[0:CROWS]

    column = columns(got("cidx"), me, plan)
    weight = got("cw")
    dist = got("cd")
    sin_t, cos_t = sine_cosine(got("ct"))
    sin_p, cos_p = sine_cosine(got("cp"))
    colb[0:PAIRS, :] = column
    values = (
        weight,
        jnp.log(RADIUS_SCALE / dist),
        weight / (dist * dist * dist),
        sin_t * cos_p,
        sin_t * sin_p,
        cos_t,
    )
    for v, value in enumerate(values):
        pk[v, 0:PAIRS, :] = value

    def packed_of(load):
        out = load(0)
        for j in range(1, GROUPS):
            out = jnp.where(group8 == j, rolled(load(GROUPS * j), BORDER * j), out)
        return out

    column_p = packed_of(lambda r: colb[r:r + 8, :])
    value_p = [packed_of(lambda r, v=v: pk[v, r:r + 8, :]) for v in range(len(values))]

    in_own = (column >= 0) & (column < LANES)
    weight_own = jnp.where(in_own, weight, 0.0)
    lanes_own = column & (LANES - 1)
    weight_rem = jnp.where(column_p >= LANES, value_p[0], 0.0)
    lanes_rem = column_p & (LANES - 1)
    tile_rem = column_p >> 7

    def spread(row, rows):
        return jnp.broadcast_to(row, (rows, LANES))

    pl.semaphore_wait(barrier, number)
    start(c_bufs, 0)

    row128 = lax.broadcasted_iota(jnp.int32, (LANES, LANES), 0)
    for k in range(PAIRS):
        wr[k] = jnp.exp(degrees * spread(values[1][k:k + 1], CROWS)) * spread(weight_own[k:k + 1], CROWS)
        ohown[:, k * LANES:(k + 1) * LANES] = jnp.where(row128 == spread(column[k:k + 1], LANES), 1.0, 0.0).astype(BF16)
        for c in range(3):
            edir[k, c:c + 1, :] = values[3 + c][k:k + 1]
    for g in range(GROUPS):
        wrp[g] = jnp.exp(degrees * spread(value_p[1][g:g + 1], CROWS)) * spread(weight_rem[g:g + 1], CROWS)
        for t in range(plan.tiles):
            ohrem[t * LANES:(t + 1) * LANES, g * LANES:(g + 1) * LANES] = jnp.where(
                row128 + (t + 1) * LANES == spread(column_p[g:g + 1], LANES), 1.0, 0.0
            ).astype(BF16)
        for c in range(3):
            edirp[g, c:c + 1, :] = value_p[3 + c][g:g + 1]

    tcol = columns(got("tidx"), me, plan)
    apart = got("td")
    cubed = apart * apart * apart
    screen = jnp.exp(-THOLE_DAMPING * cubed)
    scaled = got("tw") / cubed
    lam3 = scaled * (1.0 - screen)
    lam5 = 3.0 * scaled * (1.0 - (1.0 + THOLE_DAMPING * cubed) * screen)
    sin_t, cos_t = sine_cosine(got("tt"))
    sin_p, cos_p = sine_cosine(got("tp"))
    polar = live * got("polar")
    for v, value in enumerate((
        sin_t * cos_p, sin_t * sin_p, cos_t, lam3, lam5,
    )):
        thc[v] = value
    tlanes = tcol & (LANES - 1)
    ttile = tcol >> 7

    def moment_fields(s):
        put_columns(cs[...])
        out = jnp.dot(htm[...], point_values(), preferred_element_type=F32)
        moment = out[0:8, 0:LANES] + out[0:8, LANES:] + out[8:, 0:LANES]
        packed = jnp.where(group8 == 0, moment, 0.0)
        wide = packed
        for j in range(1, GROUPS):
            wide = wide + rolled(packed, BORDER * j)

        def field(e, strength, m):
            along = jnp.sum(e * m, axis=0, keepdims=True)
            f = strength * (3.0 * e * along - m)
            high = f.astype(BF16).astype(F32)
            return jnp.concatenate([high, f - high], axis=0).astype(BF16)

        for k in range(PAIRS):
            fown[:, k * LANES:(k + 1) * LANES] = field(edir[k], values[2][k:k + 1], moment)
        for g in range(GROUPS):
            frem[:, g * LANES:(g + 1) * LANES] = field(edirp[g], value_p[2][g:g + 1], wide)
        turn = (((1,), (1,)), ((), ()))
        away = lax.dot_general(frem[...], ohrem[...], turn, preferred_element_type=F32)
        dip_rows = pltpu.roll(ds[...], 3, 0)
        for t in range(plan.tiles):
            part = away[:, t * LANES:(t + 1) * LANES]
            fdbuf[s, t] = jnp.where(iota8 < 3, part[0:8] + part[8:], dip_rows)
        start(f_bufs, s)
        mine = lax.dot_general(fown[...], ohown[...], turn, preferred_element_type=F32)
        return mine[0:8] + mine[8:]

    def put_columns(z):
        high, low = split(z)
        for base in (0, LANES):
            zs[base:base + ROWS, 0:LANES] = high
            zs[base:base + ROWS, LANES:] = low

    def point_values():
        out = jnp.dot(hk[...], zs[...], preferred_element_type=F32)
        high, low = split((out[:, 0:LANES] + out[:, LANES:]) * ind[...])
        ws[0:GRID_PAD, 0:LANES] = high
        ws[0:GRID_PAD, LANES:] = low
        return ws[...]

    for s in range(ITERS):
        own_field = moment_fields(s)

        table = cs[0:CROWS, :]
        coupled = jnp.zeros((CROWS, LANES), F32)
        for k in range(PAIRS):
            coupled = coupled + wr[k] * lane_take(table, spread(lanes_own[k:k + 1], CROWS))
        arrive(c_bufs, s)
        for t in range(plan.tiles):
            for j in range(GROUPS):
                block = jnp.zeros((PACK, LANES), F32)
                for m in range(GROUPS):
                    slot = GROUPS * t + m
                    if slot >= plan.count or slot == plan.own:
                        continue
                    block = jnp.where(group24 == m, rolled(cbuf[s, slot], BORDER * (m - j)), block)
                pool[t, j * PACK:(j + 1) * PACK, :] = block
        far = jnp.zeros((CROWS, LANES), F32)
        for g in range(GROUPS):
            lanes = spread(lanes_rem[g:g + 1], CROWS)
            tiles = spread(tile_rem[g:g + 1], CROWS)
            found = lane_take(pool[0, 0:CROWS, :], lanes)
            for t in range(1, plan.tiles):
                found = jnp.where(tiles == t + 1, lane_take(pool[t, 0:CROWS, :], lanes), found)
            far = far + wrp[g] * found
        far = far + rolled(far, 64)
        far = far + rolled(far, 32)
        coupled = coupled + jnp.where(lane_group((CROWS, LANES)) == 0, far, 0.0)

        put_columns(jnp.concatenate([coupled, zero8], axis=0))
        inj[1:4, :] = INJECT_SCALE * ds[0:3, :]
        out = jnp.dot(ht[...], point_values(), preferred_element_type=F32)
        projected = out[0:ROWS, 0:LANES] + out[0:ROWS, LANES:] + out[ROWS:, 0:LANES]
        fresh = gain * (src[...] + inj[...] - projected)
        if s < ITERS - 1:
            cs[...] = fresh
            pack_coefs(s + 1)
            start(c_bufs, s + 1)
        else:
            coef_out[:, 0, :] = fresh[0:COEF]

        arrive(f_bufs, s)
        reaction = own_field
        for m in range(GROUPS):
            total = None
            for slot in plan.others:
                if plan.mirror(slot) % GROUPS == m:
                    total = fdrecv[s, slot] if total is None else total + fdrecv[s, slot]
            if total is not None:
                reaction = reaction + jnp.where(group8 == 0, rolled(total, -BORDER * m), 0.0)
        tables = [pltpu.roll(ds[...], 3, 0)]
        for t in range(plan.tiles):
            block = zero8
            for m in range(GROUPS):
                slot = GROUPS * t + m
                if slot >= plan.count or slot == plan.own:
                    continue
                block = jnp.where(group8 == m, rolled(fdrecv[s, slot], BORDER * m), block)
            tables.append(block)
        partner = []
        for c in range(3):
            found = jnp.zeros((PAIRS, LANES), F32)
            for t, block in enumerate(tables):
                found = jnp.where(ttile == t, lane_take(spread(block[3 + c:4 + c], PAIRS), tlanes), found)
            partner.append(found)
        along = thc[4] * (thc[0] * partner[0] + thc[1] * partner[1] + thc[2] * partner[2])
        for c in range(3):
            tmp[c:c + 1, :] = jnp.sum(thc[c] * along - thc[3] * partner[c], axis=0, keepdims=True)
        moved = polar * (ext[...] + tmp[...] + reaction)
        moved = jnp.where(iota8 < 3, moved, 0.0)
        if s < ITERS - 1:
            ds[...] = moved
        else:
            dip_out[:, 0, :] = moved[0:3]

    for s in range(ITERS):
        sent(c_bufs, s)
        sent(f_bufs, s)


def rows_of(x):
    shape = (x.shape[0], x.shape[-1]) if x.shape[0] % 8 == 0 else (x.shape[0], 1, x.shape[-1])
    return x.reshape(shape)


def local(plan, *args):
    (coef, dip, source, ind, polar, ext, counts, cidx, cw, cd, ct, cp,
     tidx, tw, td, tt, tp, harm, leb) = args
    flat = [rows_of(x) for x in (coef, dip, source, ind, cidx, cw, cd, ct, cp, tidx, tw, td, tt, tp, ext)]
    flat += [polar.reshape(1, LANES), harm.T, leb, counts]
    vmem = pl.BlockSpec(memory_space=pltpu.VMEM)
    held = [pltpu.VMEM(x.shape, x.dtype) for x in flat]
    scratch = [
        ((ROWS, LANES), F32), ((8, LANES), F32), ((ROWS, LANES), F32), ((ROWS, LANES), F32),
        ((8, LANES), F32), ((8, LANES), F32),
        ((ITERS, PACK, LANES), F32), ((ITERS, plan.count, PACK, LANES), F32),
        ((ITERS, plan.tiles, 8, LANES), F32), ((ITERS, plan.count, 8, LANES), F32),
        ((24, LANES), jnp.int32), ((6, 24, LANES), F32),
        ((PAIRS, CROWS, LANES), F32), ((GROUPS, CROWS, LANES), F32),
        ((PAIRS, 8, LANES), F32), ((GROUPS, 8, LANES), F32), ((8, LANES), F32),
        ((LANES, PAIRS * LANES), BF16), ((plan.tiles * LANES, GROUPS * LANES), BF16),
        ((16, PAIRS * LANES), BF16), ((16, GROUPS * LANES), BF16),
        ((GRID_PAD, 2 * LANES), BF16), ((2 * ROWS, GRID_K), BF16), ((16, GRID_K), BF16),
        ((LANES, GRID_K), F32), ((8, GRID_K), F32),
        ((2 * LANES, 2 * LANES), BF16), ((GRID_K, 2 * LANES), BF16), ((GRID_PAD, LANES), F32),
        ((5, PAIRS, LANES), F32), ((plan.tiles, ROWS, LANES), F32),
    ]
    semaphores = [pltpu.SemaphoreType.DMA((ITERS, plan.count))] * 4 + [pltpu.SemaphoreType.DMA((len(flat),))]
    coef_new, dip_new = pl.pallas_call(
        functools.partial(kernel, plan),
        out_shape=(pltpu.VMEM((COEF, 1, LANES), F32), pltpu.VMEM((3, 1, LANES), F32)),
        in_specs=[pl.BlockSpec(memory_space=pltpu.HBM)] * len(flat),
        out_specs=(vmem, vmem),
        scratch_shapes=held + [pltpu.VMEM(shape, kind) for shape, kind in scratch] + semaphores,
        compiler_params=pltpu.CompilerParams(
            collective_id=0, has_side_effects=True, vmem_limit_bytes=60 * 1024 * 1024
        ),
    )(*flat)
    return coef_new.reshape(coef.shape), dip_new.reshape(dip.shape)


def solution(mesh):
    plan = Slots(tuple(mesh.shape[a] for a in AXES))
    lead = P(None, ("grp", "gx"), "gy", "gz", None)
    flat = P(("grp", "gx"), "gy", "gz", None)
    in_specs = (lead,) * 4 + (flat, lead, P(("grp", "gx"), "gy", "gz")) + (lead,) * 10 + (P(), P())
    return jax.shard_map(
        functools.partial(local, plan), mesh=mesh, in_specs=in_specs, out_specs=(lead, lead), check_vma=False
    )
```
